512 devices in a mesh: particle: 64 (over z, y), fsdp: 8 (over x, core).
Axes of the slice: x: 4, y: 4, z: 16, core: 2. Of those that a mesh axis runs over, the one named last changes fastest.
Arguments:
- particles: float32 [64, 256, 2048], P('particle', 'fsdp'), may hold values from -4.4 to 4.4, as said below
- gradients: float32 [64, 256, 2048], P('particle', 'fsdp'), may hold values from -0.0008544922 to 0.0008544922
- first_moment: float32 [64, 256, 2048], P('particle', 'fsdp'), may hold values from -0.00030517578 to 0.00030517578
- second_moment: float32 [64, 256, 2048], P('particle', 'fsdp'), may hold values from 9.094947e-13 to 9.094947e-11
- spread: float32 [], replicated, may hold values from 0.06 to 0.2
Outputs:
- new_particles: float32 [64, 256, 2048], P('particle', 'fsdp')
- new_first: float32 [64, 256, 2048], P('particle', 'fsdp')
- new_second: float32 [64, 256, 2048], P('particle', 'fsdp')
- direction: float32 [64, 256, 2048], P('particle', 'fsdp')
The draws below stay inside these ranges and needn't reach their ends.
Inputs may be any that keep to these rules, and one draw needn't show every extreme that they name: `particles`: Real-valued parameters of each particle.
All inputs are finite; a program needn't handle non-finite values.
Results may differ from the reference program's by a relative error of at most 0.00015.
Values sent between devices are 32-bit elements; how exact they have to be, the bound alone decides.
No kernel may reach another device: no remote copies, remote signals or barrier semaphores. Data moves between devices by JAX's collectives and lax.ppermute only.
A program may use at most 64 MiB of HBM per device.

```python
import math
import jax
import jax.numpy as jnp
from jax import lax

COLS = 2048
ADAM_STEP = 10
ROWS = 256
PARTICLES = 64


def draw_particles(key, part):
    key = jax.random.fold_in(key, 11)
    key_coeff, key_base, key_noise = jax.random.split(key, 3)
    groups = 8
    coeff = jax.random.uniform(key_coeff, (PARTICLES, groups), jnp.float32)
    base = jax.random.truncated_normal(key_base, -4.0, 4.0, (ROWS, COLS), jnp.float32)
    noise = 0.1 * jax.random.truncated_normal(key_noise, -4.0, 4.0, (PARTICLES, ROWS, COLS), jnp.float32)
    column = jnp.arange(COLS) % groups
    weights = coeff[:, column]
    return weights[:, None, :] * base[None, :, :] + noise


def levels(key, shape, cuts, low, largest):
    level = 1.0
    for dim, blocks in cuts:
        draws = jax.random.uniform(jax.random.fold_in(jax.random.fold_in(key, 6), dim), (blocks,), jnp.float32, low / len(cuts), largest / len(cuts))
        level = level * jnp.repeat(jnp.exp(draws), shape[dim] // blocks).reshape((-1,) + (1,) * (len(shape) - 1 - dim))
    return level


def scatter_about(key, extent, width, most, shards=(), held_as=jnp.bfloat16):
    level = levels(key, extent, shards, -0.22, 0.18) if shards else 1.0
    values = jax.random.normal(key, extent, jnp.float32) * width * level
    return jnp.minimum(jnp.maximum(values, -most), most).astype(held_as)


def setup_inputs(seed: int = 0) -> dict:
    seeds = jax.random.split(jax.random.key(seed), 6)
    particles = draw_particles(jax.random.fold_in(seeds[5], 71), 0)
    gradients = scatter_about(seeds[1], (PARTICLES, ROWS, COLS), (30.0 / (ROWS * COLS)), 0.0008544922, ((0, 64), (1, 8)), jnp.float32)
    first_moment = scatter_about(seeds[2], (PARTICLES, ROWS, COLS), (10.0 / (ROWS * COLS)), 0.00030517578, ((0, 64), (1, 8)), jnp.float32)
    second_moment = jnp.clip(jnp.exp(math.log(9.094947017729282e-11) - 4.6051702 * jax.random.uniform(seeds[3], (PARTICLES, ROWS, COLS), jnp.float32) ** levels(seeds[3], (PARTICLES, ROWS, COLS), ((0, 64), (1, 8)), -0.2, 0.2)), 9.094947017729282e-13, 9.094947017729282e-11)
    spread = jnp.clip(jnp.exp(jax.random.uniform(seeds[4], (), jnp.float32, math.log(0.06), math.log(0.2))), 0.06, 0.2)
    return {"particles": particles, "gradients": gradients, "first_moment": first_moment, "second_moment": second_moment, "spread": spread}


beta_one = 0.9
beta_two = 0.999
learn_rate = 0.05
adam_eps = 1e-08

def kernel_of(gram, spread, total):
    diag = jnp.diagonal(gram)
    dist = diag[:, None] + diag[None, :] - 2.0 * gram
    return jnp.exp(-dist / (spread * total))

def mix(kernel, flat_x, flat_g, spread, total, count):
    rowsum = lax.optimization_barrier(jnp.sum(kernel, axis=1))
    pulled = jnp.dot(kernel, flat_g, precision=lax.Precision.HIGHEST, preferred_element_type=jnp.float32)
    kx = jnp.dot(kernel, flat_x, precision=lax.Precision.HIGHEST, preferred_element_type=jnp.float32)
    push = 2.0 / (spread * total) * (rowsum[:, None] * flat_x - kx)
    return (pulled + push) / count

def adam_update(params, direction, first, second):
    new_first = beta_one * first + (1.0 - beta_one) * direction
    new_second = beta_two * second + (1.0 - beta_two) * direction * direction
    first_hat = new_first / (1.0 - beta_one ** ADAM_STEP)
    second_hat = new_second / (1.0 - beta_two ** ADAM_STEP)
    return (params + learn_rate * first_hat / (jnp.sqrt(second_hat) + adam_eps), new_first, new_second)

def reference(particles, gradients, first_moment, second_moment, spread):
    count = particles.shape[0]
    flat_x = particles.reshape(count, -1)
    flat_g = gradients.reshape(count, -1)
    total = flat_x.shape[1]
    gram = jnp.dot(flat_x, flat_x.T, precision=lax.Precision.HIGHEST, preferred_element_type=jnp.float32)
    kernel = kernel_of(gram, spread, total)
    direction = mix(kernel, flat_x, flat_g, spread, total, count).reshape(particles.shape)
    new_x, new_m, new_v = adam_update(particles, direction, first_moment, second_moment)
    return (new_x, new_m, new_v, direction)
```

```python
import functools

import jax
import jax.numpy as jnp
from jax import lax
from jax.experimental import pallas as pl
from jax.experimental.pallas import tpu as pltpu
from jax.sharding import Mesh, PartitionSpec as P

ADAM_STEP = 10

beta_one = 0.9
beta_two = 0.999
learn_rate = 0.05
adam_eps = 1e-08

COUNT = 64
HALF = COUNT // 2
SUB, LANE = 8, 128
PACK = 16

PLANE = ("y", "x", "core")
RING = ("z", "y")


def dot(a, b, dims):
    return lax.dot_general(
        a, b, (dims, ((), ())),
        precision=lax.Precision.HIGHEST, preferred_element_type=jnp.float32,
    )


def iota(shape, dim):
    return lax.broadcasted_iota(jnp.int32, shape, dim)


def dist_kernel(slab_ref, out_ref):
    x = jnp.concatenate([slab_ref[:, s, :] for s in range(SUB)], axis=1)
    gram = dot(x, jnp.concatenate([x, x], axis=0), ((1,), (1,)))
    lane = lax.rem(iota((COUNT, LANE), 1), COUNT)
    on_diag = jnp.where(lane == iota((COUNT, LANE), 0), gram, 0.0)
    norm_row = jnp.sum(on_diag, axis=0, keepdims=True)
    norm_col = 0.5 * jnp.sum(on_diag, axis=1, keepdims=True)
    dist = norm_col + norm_row - 2.0 * gram
    top = dist[:HALF]
    low = pltpu.roll(dist[HALF:], LANE - HALF, 1)
    lane = lax.rem(iota((HALF, LANE), 1), COUNT)
    keep = lane > iota((HALF, LANE), 0)
    both = jnp.where(keep, top, low)
    packed = jnp.where(iota((PACK, LANE), 1) < COUNT, both[:PACK], both[PACK:])
    for k in range(out_ref.shape[0]):
        out_ref[k] = packed


def sum_kernel(in_ref, out_ref):
    total = jnp.sum(in_ref[...], axis=0)
    for k in range(out_ref.shape[0]):
        out_ref[k] = total


def mix_kernel(entries, spread_ref, dist_ref, slab_ref, out_ref):
    packed = jnp.sum(dist_ref[...], axis=0)
    width = spread_ref[0] * entries
    packed = jnp.exp(-packed / width)
    both = jnp.concatenate([packed, pltpu.roll(packed, COUNT, 1)], axis=0)
    lane, row = iota((HALF, LANE), 1), iota((HALF, LANE), 0)
    top = jnp.where((lane > row) & (lane < COUNT), both, 0.0)
    low = jnp.where((lane >= HALF) & (lane - HALF < row), pltpu.roll(both, HALF, 1), 0.0)
    half = jnp.concatenate([top, low, jnp.zeros((LANE - COUNT, LANE), jnp.float32)], axis=0)
    eye = jnp.where(iota((LANE, LANE), 0) == iota((LANE, LANE), 1), 1.0, 0.0)
    kernel = (half + half.T + eye)[:COUNT, :COUNT]
    rowsum = jnp.sum(kernel, axis=1, keepdims=True)
    pull = 2.0 / jnp.full((COUNT, 1), width, jnp.float32)
    own = pull * rowsum
    x = jnp.concatenate([slab_ref[:, s, :] for s in range(SUB)], axis=1)
    g = jnp.concatenate([slab_ref[:, SUB + s, :] for s in range(SUB)], axis=1)
    mixed = dot(kernel, g - pull * x, ((1,), (0,)))
    mixed = (mixed + own * x) * (1.0 / COUNT)
    for s in range(SUB):
        out_ref[:, s, :] = mixed[:, s * LANE:(s + 1) * LANE]


def whole(count):
    return [pl.BlockSpec(memory_space=pltpu.VMEM)] * count


def tiles(block):
    rows, cols = block.shape
    return (
        block.reshape(rows // SUB, SUB, cols // LANE, LANE)
        .transpose(0, 2, 1, 3)
        .reshape(-1, SUB, LANE)
    )


def untiles(parts, rows, cols):
    return (
        parts.reshape(rows // SUB, cols // LANE, SUB, LANE)
        .transpose(0, 2, 1, 3)
        .reshape(rows, cols)
    )


def exchange(array, axes):
    return lax.all_to_all(array, axes, split_axis=0, concat_axis=0, tiled=True)


def body(particles, gradients, first_moment, second_moment, spread):
    _, rows, cols = particles.shape
    entries = rows * cols * lax.axis_size("x") * lax.axis_size("core")
    plane = lax.axis_size("y") * lax.axis_size("x") * lax.axis_size("core")
    depth = lax.axis_size("z")
    with jax.named_scope("gather_slab"):
        both = jnp.concatenate([tiles(particles[0]), tiles(gradients[0])], axis=1)
        slab = exchange(both, RING)
    with jax.named_scope("distances"):
        part = pl.pallas_call(
            dist_kernel,
            out_shape=jax.ShapeDtypeStruct((plane, PACK, LANE), jnp.float32),
            in_specs=whole(1),
            out_specs=whole(1)[0],
        )(slab)
        part = exchange(part, PLANE)
        part = pl.pallas_call(
            sum_kernel,
            out_shape=jax.ShapeDtypeStruct((depth, PACK, LANE), jnp.float32),
            in_specs=whole(1),
            out_specs=whole(1)[0],
        )(part)
        part = exchange(part, "z")
    with jax.named_scope("mix"):
        mixed = pl.pallas_call(
            functools.partial(mix_kernel, float(entries)),
            out_shape=jax.ShapeDtypeStruct((COUNT, SUB, LANE), jnp.float32),
            in_specs=[pl.BlockSpec(memory_space=pltpu.SMEM)] + whole(2),
            out_specs=whole(1)[0],
        )(spread.reshape(1), part, slab)
    with jax.named_scope("return_slab"):
        direction = untiles(exchange(mixed, RING), rows, cols)[None]
    with jax.named_scope("adam"):
        new_first = beta_one * first_moment + (1.0 - beta_one) * direction
        new_second = beta_two * second_moment + (1.0 - beta_two) * direction * direction
        first_hat = new_first / (1.0 - beta_one**ADAM_STEP)
        second_hat = new_second / (1.0 - beta_two**ADAM_STEP)
        new_params = particles + learn_rate * first_hat / (jnp.sqrt(second_hat) + adam_eps)
    return (new_params, new_first, new_second, direction)


def solution(mesh):
    split = Mesh(mesh.devices.reshape(16, 4, 4, 2), ("z", "y", "x", "core"))
    block = P(("z", "y"), ("x", "core"), None)
    return jax.shard_map(
        body,
        mesh=split,
        in_specs=(block, block, block, block, P()),
        out_specs=(block, block, block, block),
        check_vma=False,
    )
```

```python
import jax
import jax.numpy as jnp
from jax import lax
from jax.experimental import pallas as pl
from jax.experimental.pallas import tpu as pltpu
from jax.sharding import Mesh, PartitionSpec as P

ADAM_STEP = 10

beta_one = 0.9
beta_two = 0.999
learn_rate = 0.05
adam_eps = 1e-08

COUNT = 64
HALF = COUNT // 2
SUB, LANE = 8, 128
CHUNKS = 4
PACK = 16

PLANE = ("y", "x", "core")
RING = ("z", "y")


def dot(a, b, dims):
    return lax.dot_general(
        a, b, (dims, ((), ())),
        precision=lax.Precision.HIGHEST, preferred_element_type=jnp.float32,
    )


def iota(shape, dim):
    return lax.broadcasted_iota(jnp.int32, shape, dim)


def stack_kernel(x_ref, g_ref, out_ref, sems):
    copies = [
        pltpu.make_async_copy(x_ref, out_ref.at[:, pl.ds(0, SUB), :], sems.at[0]),
        pltpu.make_async_copy(g_ref, out_ref.at[:, pl.ds(SUB, SUB), :], sems.at[1]),
    ]
    for copy in copies:
        copy.start()
    for copy in copies:
        copy.wait()


def dist_kernel(slab_ref, out_ref):
    x = jnp.concatenate([slab_ref[:, s, :] for s in range(SUB)], axis=1)
    gram = dot(x, jnp.concatenate([x, x], axis=0), ((1,), (1,)))
    lane = lax.rem(iota((COUNT, LANE), 1), COUNT)
    on_diag = jnp.where(lane == iota((COUNT, LANE), 0), gram, 0.0)
    norm_row = jnp.sum(on_diag, axis=0, keepdims=True)
    norm_col = 0.5 * jnp.sum(on_diag, axis=1, keepdims=True)
    dist = norm_col + norm_row - 2.0 * gram
    top = dist[:HALF]
    low = pltpu.roll(dist[HALF:], LANE - HALF, 1)
    lane = lax.rem(iota((HALF, LANE), 1), COUNT)
    keep = lane > iota((HALF, LANE), 0)
    both = jnp.where(keep, top, low)
    packed = jnp.where(iota((PACK, LANE), 1) < COUNT, both[:PACK], both[PACK:])
    for k in range(out_ref.shape[0]):
        out_ref[k] = packed


def sum_kernel(in_ref, out_ref):
    total = jnp.sum(in_ref[...], axis=0)
    for k in range(out_ref.shape[0]):
        out_ref[k] = total


def mix_kernel(width_ref, dist_ref, slab_ref, out_ref):
    packed = jnp.exp(-jnp.sum(dist_ref[...], axis=0) / width_ref[0:1])
    both = jnp.concatenate([packed, pltpu.roll(packed, COUNT, 1)], axis=0)
    lane, row = iota((HALF, LANE), 1), iota((HALF, LANE), 0)
    top = jnp.where((lane > row) & (lane < COUNT), both, 0.0)
    low = jnp.where((lane >= HALF) & (lane - HALF < row), pltpu.roll(both, HALF, 1), 0.0)
    half = jnp.concatenate([top, low, jnp.zeros((LANE - COUNT, LANE), jnp.float32)], axis=0)
    eye = jnp.where(iota((LANE, LANE), 0) == iota((LANE, LANE), 1), 1.0, 0.0)
    kernel = (half + half.T + eye)[:COUNT, :COUNT]
    rowsum = jnp.sum(kernel, axis=1, keepdims=True)
    pull = 2.0 / width_ref[0:1, 0:1]
    own = pull * rowsum
    x = jnp.concatenate([slab_ref[:, s, :] for s in range(SUB)], axis=1)
    g = jnp.concatenate([slab_ref[:, SUB + s, :] for s in range(SUB)], axis=1)
    mixed = dot(kernel, g - pull * x, ((1,), (0,)))
    mixed = (mixed + own * x) * (1.0 / COUNT)
    for s in range(SUB):
        out_ref[:, s, :] = mixed[:, s * LANE:(s + 1) * LANE]


def adam_kernel(x_ref, m_ref, v_ref, d_ref, new_x, new_m, new_v, new_d, out_x, out_m, out_v, sems):
    copies = [pltpu.make_async_copy(d_ref, new_d, sems.at[0])]
    copies[0].start()
    rows = x_ref.shape[0] // CHUNKS
    for k in range(CHUNKS):
        part = pl.ds(k * rows, rows)
        direction = d_ref[part]
        first = beta_one * m_ref[part] + (1.0 - beta_one) * direction
        second = beta_two * v_ref[part] + (1.0 - beta_two) * direction * direction
        out_m[part] = first
        out_v[part] = second
        first_hat = first / (1.0 - beta_one**ADAM_STEP)
        second_hat = second / (1.0 - beta_two**ADAM_STEP)
        out_x[part] = x_ref[part] + learn_rate * first_hat / (jnp.sqrt(second_hat) + adam_eps)
        for i, (src, dst) in enumerate(((out_m, new_m), (out_v, new_v), (out_x, new_x))):
            copy = pltpu.make_async_copy(src.at[part], dst.at[part], sems.at[1 + 3 * k + i])
            copy.start()
            copies.append(copy)
    for copy in copies:
        copy.wait()


IN_VMEM = pl.BlockSpec(memory_space=pltpu.VMEM)
ANYWHERE = pl.BlockSpec(memory_space=pl.ANY)


def call(kernel, out_shape, in_specs, args, out_specs=IN_VMEM, scratch=()):
    args = [
        pltpu.with_memory_space_constraint(a, pltpu.VMEM if s is IN_VMEM else pltpu.HBM)
        for a, s in zip(args, in_specs)
    ]
    return pl.pallas_call(
        kernel, out_shape=out_shape, in_specs=in_specs, out_specs=out_specs, scratch_shapes=list(scratch)
    )(*args)


def vmem(*shape):
    return pltpu.VMEM(shape, jnp.float32)


def tiles(block):
    rows, cols = block.shape
    return (
        block.reshape(rows // SUB, SUB, cols // LANE, LANE)
        .transpose(0, 2, 1, 3)
        .reshape(-1, SUB, LANE)
    )


def untiles(parts, rows, cols):
    return (
        parts.reshape(rows // SUB, cols // LANE, SUB, LANE)
        .transpose(0, 2, 1, 3)
        .reshape(rows, cols)
    )


def exchange(array, axes):
    return lax.all_to_all(array, axes, split_axis=0, concat_axis=0, tiled=True)


def body(particles, gradients, first_moment, second_moment, spread):
    _, rows, cols = particles.shape
    entries = rows * cols * lax.axis_size("x") * lax.axis_size("core")
    plane = lax.axis_size("y") * lax.axis_size("x") * lax.axis_size("core")
    depth = lax.axis_size("z")
    with jax.named_scope("gather_slab"):
        both = call(
            stack_kernel, vmem(COUNT, 2 * SUB, LANE), [ANYWHERE] * 2,
            (tiles(particles[0]), tiles(gradients[0])),
            scratch=[pltpu.SemaphoreType.DMA((2,))],
        )
        slab = exchange(both, RING)
    with jax.named_scope("distances"):
        part = call(dist_kernel, vmem(plane, PACK, LANE), [IN_VMEM], (slab,))
        part = exchange(part, PLANE)
        part = call(sum_kernel, vmem(depth, PACK, LANE), [IN_VMEM], (part,))
        part = exchange(part, "z")
    with jax.named_scope("mix"):
        width = jnp.full((SUB, LANE), spread * entries, jnp.float32)
        mixed = call(mix_kernel, vmem(COUNT, SUB, LANE), [IN_VMEM] * 3, (width, part, slab))
    with jax.named_scope("return_slab"):
        direction = untiles(exchange(mixed, RING), rows, cols)
    with jax.named_scope("adam"):
        block = jax.ShapeDtypeStruct((rows, cols), jnp.float32)
        outs = call(
            adam_kernel, (block,) * 4, [IN_VMEM] * 4,
            (particles[0], first_moment[0], second_moment[0], direction),
            out_specs=(ANYWHERE,) * 4,
            scratch=[vmem(rows, cols)] * 3 + [pltpu.SemaphoreType.DMA((1 + 3 * CHUNKS,))],
        )
    return tuple(out[None] for out in outs)


def solution(mesh):
    split = Mesh(mesh.devices.reshape(16, 4, 4, 2), ("z", "y", "x", "core"))
    block = P(("z", "y"), ("x", "core"), None)
    return jax.shard_map(
        body,
        mesh=split,
        in_specs=(block, block, block, block, P()),
        out_specs=(block, block, block, block),
        check_vma=False,
    )
```

```python
import jax
import jax.numpy as jnp
from jax import lax
from jax.experimental import pallas as pl
from jax.experimental.pallas import tpu as pltpu
from jax.sharding import Mesh, PartitionSpec as P

ADAM_STEP = 10

beta_one = 0.9
beta_two = 0.999
learn_rate = 0.05
adam_eps = 1e-08

COUNT = 64
HALF = COUNT // 2
SUB, LANE = 8, 128
CHUNKS = 4
PACK = 16
PACKED = PACK // SUB

PLANE = ("y", "x")
RING = ("z", "y")


def dot(a, b, dims):
    return lax.dot_general(
        a, b, (dims, ((), ())),
        precision=lax.Precision.HIGHEST, preferred_element_type=jnp.float32,
    )


def iota(shape, dim):
    return lax.broadcasted_iota(jnp.int32, shape, dim)


def pack_kernel(width_ref, slab_ref, g_ref, out_ref, sem):
    copy = pltpu.make_async_copy(g_ref, out_ref.at[pl.ds(PACKED, COUNT)], sem)
    copy.start()
    x = jnp.concatenate([slab_ref[:, s, :] for s in range(SUB)], axis=1)
    gram = dot(x, jnp.concatenate([x, x], axis=0), ((1,), (1,)))
    lane = lax.rem(iota((COUNT, LANE), 1), COUNT)
    on_diag = jnp.where(lane == iota((COUNT, LANE), 0), gram, 0.0)
    norm_row = jnp.sum(on_diag, axis=0, keepdims=True)
    norm_col = 0.5 * jnp.sum(on_diag, axis=1, keepdims=True)
    dist = norm_col + norm_row - 2.0 * gram
    top = dist[:HALF]
    low = pltpu.roll(dist[HALF:], LANE - HALF, 1)
    lane = lax.rem(iota((HALF, LANE), 1), COUNT)
    keep = lane > iota((HALF, LANE), 0)
    both = jnp.where(keep, top, low)
    packed = jnp.where(iota((PACK, LANE), 1) < COUNT, both[:PACK], both[PACK:]) / width_ref[0:1]
    for k in range(PACKED):
        out_ref[k] = packed[k * SUB:(k + 1) * SUB]
    copy.wait()


def spread_kernel(both_ref, out_ref):
    total = both_ref[0, 0:PACKED] + both_ref[1, 0:PACKED]
    for k in range(out_ref.shape[0]):
        out_ref[k] = total


def stack_kernel(both_ref, out_ref):
    out_ref[:, 0:SUB, :] = both_ref[0, PACKED:]
    out_ref[:, SUB:, :] = both_ref[1, PACKED:]


def last_kernel(in_ref, out_ref, kept_ref):
    out_ref[0:PACKED] = jnp.sum(in_ref[...], axis=0)
    out_ref[PACKED:] = jnp.zeros((COUNT, SUB, LANE), jnp.float32)
    kept_ref[...] = jnp.zeros((COUNT, SUB, LANE), jnp.float32)


def split_kernel(in_ref, out_ref, kept_ref):
    out_ref[0:PACKED] = jnp.zeros((PACKED, SUB, LANE), jnp.float32)
    out_ref[PACKED:] = in_ref[:, 0:SUB, :]
    kept_ref[...] = in_ref[:, SUB:, :]


def sum_kernel(in_ref, out_ref):
    total = jnp.sum(in_ref[...], axis=0)
    for k in range(out_ref.shape[0]):
        out_ref[k] = total


def mix_kernel(core_ref, width_ref, both_ref, kept_ref, slab_ref, out_ref):
    packed = jnp.exp(-both_ref[0, 0:PACKED].reshape(PACK, LANE))
    both = jnp.concatenate([packed, pltpu.roll(packed, COUNT, 1)], axis=0)
    lane, row = iota((HALF, LANE), 1), iota((HALF, LANE), 0)
    top = jnp.where((lane > row) & (lane < COUNT), both, 0.0)
    low = jnp.where((lane >= HALF) & (lane - HALF < row), pltpu.roll(both, HALF, 1), 0.0)
    half = jnp.concatenate([top, low, jnp.zeros((LANE - COUNT, LANE), jnp.float32)], axis=0)
    eye = jnp.where(iota((LANE, LANE), 0) == iota((LANE, LANE), 1), 1.0, 0.0)
    kernel = (half + half.T + eye)[:COUNT, :COUNT]
    rowsum = jnp.sum(kernel, axis=1, keepdims=True)
    pull = 2.0 / width_ref[0:1, 0:1]
    own = pull * rowsum
    x = jnp.concatenate([slab_ref[:, s, :] for s in range(SUB)], axis=1)
    grads = jnp.where(core_ref[...] == 0.0, both_ref[1, PACKED:], kept_ref[...])
    g = jnp.concatenate([grads[:, s, :] for s in range(SUB)], axis=1)
    mixed = dot(kernel, g - pull * x, ((1,), (0,)))
    mixed = (mixed + own * x) * (1.0 / COUNT)
    for s in range(SUB):
        out_ref[:, s, :] = mixed[:, s * LANE:(s + 1) * LANE]


def adam_kernel(x_ref, m_ref, v_ref, d_ref, new_x, new_m, new_v, new_d, out_x, out_m, out_v, sems):
    copies = [pltpu.make_async_copy(d_ref, new_d, sems.at[0])]
    copies[0].start()
    rows = x_ref.shape[0] // CHUNKS
    for k in range(CHUNKS):
        part = pl.ds(k * rows, rows)
        direction = d_ref[part]
        first = beta_one * m_ref[part] + (1.0 - beta_one) * direction
        second = beta_two * v_ref[part] + (1.0 - beta_two) * direction * direction
        out_m[part] = first
        out_v[part] = second
        first_hat = first / (1.0 - beta_one**ADAM_STEP)
        second_hat = second / (1.0 - beta_two**ADAM_STEP)
        out_x[part] = x_ref[part] + learn_rate * first_hat / (jnp.sqrt(second_hat) + adam_eps)
        for i, (src, dst) in enumerate(((out_m, new_m), (out_v, new_v), (out_x, new_x))):
            copy = pltpu.make_async_copy(src.at[part], dst.at[part], sems.at[1 + 3 * k + i])
            copy.start()
            copies.append(copy)
    for copy in copies:
        copy.wait()


IN_VMEM = pl.BlockSpec(memory_space=pltpu.VMEM)
ANYWHERE = pl.BlockSpec(memory_space=pl.ANY)


def call(kernel, out_shape, in_specs, args, out_specs=IN_VMEM, scratch=()):
    args = [
        pltpu.with_memory_space_constraint(a, pltpu.VMEM if s is IN_VMEM else pltpu.HBM)
        for a, s in zip(args, in_specs)
    ]
    return pl.pallas_call(
        kernel, out_shape=out_shape, in_specs=in_specs, out_specs=out_specs, scratch_shapes=list(scratch)
    )(*args)


def vmem(*shape):
    return pltpu.VMEM(shape, jnp.float32)


def tiles(block):
    rows, cols = block.shape
    return (
        block.reshape(rows // SUB, SUB, cols // LANE, LANE)
        .transpose(0, 2, 1, 3)
        .reshape(-1, SUB, LANE)
    )


def untiles(parts, rows, cols):
    return (
        parts.reshape(rows // SUB, cols // LANE, SUB, LANE)
        .transpose(0, 2, 1, 3)
        .reshape(rows, cols)
    )


def exchange(array, axes):
    return lax.all_to_all(array, axes, split_axis=0, concat_axis=0, tiled=True)


def share(array):
    return lax.all_gather(array, "core", axis=0, tiled=False)


def body(particles, gradients, first_moment, second_moment, spread):
    _, rows, cols = particles.shape
    entries = rows * cols * lax.axis_size("x") * lax.axis_size("core")
    plane = lax.axis_size("y") * lax.axis_size("x")
    depth = lax.axis_size("z")
    core = lax.axis_index("core")
    width = jnp.full((SUB, LANE), spread * entries, jnp.float32)
    which = jnp.full((1, SUB, LANE), core.astype(jnp.float32), jnp.float32)
    payload = vmem(PACKED + COUNT, SUB, LANE)
    with jax.named_scope("gather_slab"):
        slab = exchange(tiles(particles[0]), RING)
    with jax.named_scope("distances"):
        both = share(call(
            pack_kernel, payload, [IN_VMEM, IN_VMEM, ANYWHERE], (width, slab, tiles(gradients[0])),
            scratch=[pltpu.SemaphoreType.DMA],
        ))

    def reduce(both):
        part = call(spread_kernel, vmem(plane, PACKED, SUB, LANE), [IN_VMEM], (both,))
        part = exchange(part, PLANE)
        part = call(sum_kernel, vmem(depth, PACKED, SUB, LANE), [IN_VMEM], (part,))
        part = exchange(part, "z")
        return call(
            last_kernel, (payload, vmem(COUNT, SUB, LANE)), [IN_VMEM], (part,), out_specs=(IN_VMEM,) * 2
        )

    def gather(both):
        grads = call(stack_kernel, vmem(COUNT, 2 * SUB, LANE), [IN_VMEM], (both,))
        grads = exchange(grads, RING)
        return call(
            split_kernel, (payload, vmem(COUNT, SUB, LANE)), [IN_VMEM], (grads,), out_specs=(IN_VMEM,) * 2
        )

    with jax.named_scope("reduce_or_gather"):
        mine, kept = lax.cond(core == 0, reduce, gather, both)
        both = share(mine)
    with jax.named_scope("mix"):
        mixed = call(
            mix_kernel, vmem(COUNT, SUB, LANE), [IN_VMEM] * 5, (which, width, both, kept, slab)
        )
    with jax.named_scope("return_slab"):
        direction = untiles(exchange(mixed, RING), rows, cols)
    with jax.named_scope("adam"):
        block = jax.ShapeDtypeStruct((rows, cols), jnp.float32)
        outs = call(
            adam_kernel, (block,) * 4, [IN_VMEM] * 4,
            (particles[0], first_moment[0], second_moment[0], direction),
            out_specs=(ANYWHERE,) * 4,
            scratch=[vmem(rows, cols)] * 3 + [pltpu.SemaphoreType.DMA((1 + 3 * CHUNKS,))],
        )
    return tuple(out[None] for out in outs)


def solution(mesh):
    split = Mesh(mesh.devices.reshape(16, 4, 4, 2), ("z", "y", "x", "core"))
    block = P(("z", "y"), ("x", "core"), None)
    return jax.shard_map(
        body,
        mesh=split,
        in_specs=(block, block, block, block, P()),
        out_specs=(block, block, block, block),
        check_vma=False,
    )
```

```python
import jax
import jax.numpy as jnp
from jax import lax
from jax.experimental import pallas as pl
from jax.experimental.pallas import tpu as pltpu
from jax.sharding import Mesh, PartitionSpec as P

ADAM_STEP = 10

beta_one = 0.9
beta_two = 0.999
learn_rate = 0.05
adam_eps = 1e-08

COUNT = 64
HALF = COUNT // 2
SUB, LANE = 8, 128
CHUNKS = 4
PACK = 16
PACKED = PACK // SUB

PLANE = ("y", "x")
RING = ("z", "y")


def dot(a, b, dims):
    return lax.dot_general(
        a, b, (dims, ((), ())),
        precision=lax.Precision.HIGHEST, preferred_element_type=jnp.float32,
    )


def iota(shape, dim):
    return lax.broadcasted_iota(jnp.int32, shape, dim)


def pack_kernel(width_ref, slab_ref, g_ref, out_ref, sem):
    copy = pltpu.make_async_copy(g_ref, out_ref.at[pl.ds(PACKED, COUNT)], sem)
    copy.start()
    x = jnp.concatenate([slab_ref[:, s, :] for s in range(SUB)], axis=1)
    gram = dot(x, jnp.concatenate([x, x], axis=0), ((1,), (1,)))
    lane = lax.rem(iota((COUNT, LANE), 1), COUNT)
    on_diag = jnp.where(lane == iota((COUNT, LANE), 0), gram, 0.0)
    norm_row = jnp.sum(on_diag, axis=0, keepdims=True)
    norm_col = 0.5 * jnp.sum(on_diag, axis=1, keepdims=True)
    dist = norm_col + norm_row - 2.0 * gram
    top = dist[:HALF]
    low = pltpu.roll(dist[HALF:], LANE - HALF, 1)
    lane = lax.rem(iota((HALF, LANE), 1), COUNT)
    keep = lane > iota((HALF, LANE), 0)
    both = jnp.where(keep, top, low)
    packed = jnp.where(iota((PACK, LANE), 1) < COUNT, both[:PACK], both[PACK:]) / width_ref[0:1]
    for k in range(PACKED):
        out_ref[k] = packed[k * SUB:(k + 1) * SUB]
    copy.wait()


def spread_kernel(both_ref, out_ref):
    total = both_ref[0, 0:PACKED] + both_ref[1, 0:PACKED]
    for k in range(out_ref.shape[0]):
        out_ref[k] = total


def stack_kernel(both_ref, out_ref):
    out_ref[:, 0:SUB, :] = both_ref[0, PACKED:]
    out_ref[:, SUB:, :] = both_ref[1, PACKED:]


def last_kernel(in_ref, out_ref, kept_ref):
    out_ref[0:PACKED] = jnp.sum(in_ref[...], axis=0)
    out_ref[PACKED:] = jnp.zeros((COUNT, SUB, LANE), jnp.float32)
    kept_ref[...] = jnp.zeros((COUNT, SUB, LANE), jnp.float32)


def split_kernel(in_ref, out_ref, kept_ref):
    out_ref[0:PACKED] = jnp.zeros((PACKED, SUB, LANE), jnp.float32)
    out_ref[PACKED:] = in_ref[:, 0:SUB, :]
    kept_ref[...] = in_ref[:, SUB:, :]


def sum_kernel(in_ref, out_ref):
    total = jnp.sum(in_ref[...], axis=0)
    for k in range(out_ref.shape[0]):
        out_ref[k] = total


def mix_kernel(core_ref, width_ref, both_ref, kept_ref, slab_ref, out_ref):
    packed = jnp.exp(-both_ref[0, 0:PACKED].reshape(PACK, LANE))
    both = jnp.concatenate([packed, pltpu.roll(packed, COUNT, 1)], axis=0)
    lane, row = iota((HALF, LANE), 1), iota((HALF, LANE), 0)
    top = jnp.where((lane > row) & (lane < COUNT), both, 0.0)
    low = jnp.where((lane >= HALF) & (lane - HALF < row), pltpu.roll(both, HALF, 1), 0.0)
    half = jnp.concatenate([top, low, jnp.zeros((LANE - COUNT, LANE), jnp.float32)], axis=0)
    eye = jnp.where(iota((LANE, LANE), 0) == iota((LANE, LANE), 1), 1.0, 0.0)
    kernel = (half + half.T + eye)[:COUNT, :COUNT]
    rowsum = jnp.sum(kernel, axis=1, keepdims=True)
    pull = 2.0 / width_ref[0:1, 0:1]
    own = pull * rowsum
    x = jnp.concatenate([slab_ref[:, s, :] for s in range(SUB)], axis=1)
    grads = jnp.where(core_ref[...] == 0.0, both_ref[1, PACKED:], kept_ref[...])
    g = jnp.concatenate([grads[:, s, :] for s in range(SUB)], axis=1)
    mixed = dot(kernel, g - pull * x, ((1,), (0,)))
    mixed = (mixed + own * x) * (1.0 / COUNT)
    for s in range(SUB):
        out_ref[:, s, :] = mixed[:, s * LANE:(s + 1) * LANE]


def adam_kernel(x_ref, m_ref, v_ref, d_ref, new_x, new_m, new_v, new_d, out_x, out_m, out_v, sems):
    copies = [pltpu.make_async_copy(d_ref, new_d, sems.at[0])]
    copies[0].start()
    rows = x_ref.shape[0] // CHUNKS
    for k in range(CHUNKS):
        part = pl.ds(k * rows, rows)
        direction = d_ref[part]
        first = beta_one * m_ref[part] + (1.0 - beta_one) * direction
        second = beta_two * v_ref[part] + (1.0 - beta_two) * direction * direction
        out_m[part] = first
        out_v[part] = second
        first_hat = first / (1.0 - beta_one**ADAM_STEP)
        second_hat = second / (1.0 - beta_two**ADAM_STEP)
        out_x[part] = x_ref[part] + learn_rate * first_hat / (jnp.sqrt(second_hat) + adam_eps)
        for i, (src, dst) in enumerate(((out_m, new_m), (out_v, new_v), (out_x, new_x))):
            copy = pltpu.make_async_copy(src.at[part], dst.at[part], sems.at[1 + 3 * k + i])
            copy.start()
            copies.append(copy)
    for copy in copies:
        copy.wait()


IN_VMEM = pl.BlockSpec(memory_space=pltpu.VMEM)
ANYWHERE = pl.BlockSpec(memory_space=pl.ANY)


def call(kernel, out_shape, in_specs, args, out_specs=IN_VMEM, scratch=()):
    args = [
        pltpu.with_memory_space_constraint(a, pltpu.VMEM if s is IN_VMEM else pltpu.HBM)
        for a, s in zip(args, in_specs)
    ]
    return pl.pallas_call(
        kernel, out_shape=out_shape, in_specs=in_specs, out_specs=out_specs, scratch_shapes=list(scratch)
    )(*args)


def vmem(*shape):
    return pltpu.VMEM(shape, jnp.float32)


def tiles(block):
    rows, cols = block.shape
    return (
        block.reshape(rows // SUB, SUB, cols // LANE, LANE)
        .transpose(0, 2, 1, 3)
        .reshape(-1, SUB, LANE)
    )


def untiles(parts, rows, cols):
    return (
        parts.reshape(rows // SUB, cols // LANE, SUB, LANE)
        .transpose(0, 2, 1, 3)
        .reshape(rows, cols)
    )


def exchange(array, axes):
    places = [0]
    for axis in axes:
        size = lax.axis_size(axis)
        places = [p * size + (i + size // 2) % size for p in places for i in range(size)]
    return lax.all_to_all(
        array, axes, split_axis=0, concat_axis=0, axis_index_groups=[places], tiled=True
    )


def share(array):
    return lax.all_gather(array, "core", axis=0, tiled=False)


def body(particles, gradients, first_moment, second_moment, spread):
    _, rows, cols = particles.shape
    entries = rows * cols * lax.axis_size("x") * lax.axis_size("core")
    plane = lax.axis_size("y") * lax.axis_size("x")
    depth = lax.axis_size("z")
    core = lax.axis_index("core")
    width = jnp.full((SUB, LANE), spread * entries, jnp.float32)
    which = jnp.full((1, SUB, LANE), core.astype(jnp.float32), jnp.float32)
    payload = vmem(PACKED + COUNT, SUB, LANE)
    with jax.named_scope("gather_slab"):
        slab = exchange(tiles(particles[0]), RING)
    with jax.named_scope("distances"):
        both = share(call(
            pack_kernel, payload, [IN_VMEM, IN_VMEM, ANYWHERE], (width, slab, tiles(gradients[0])),
            scratch=[pltpu.SemaphoreType.DMA],
        ))

    def reduce(both):
        part = call(spread_kernel, vmem(plane, PACKED, SUB, LANE), [IN_VMEM], (both,))
        part = exchange(part, PLANE)
        part = call(sum_kernel, vmem(depth, PACKED, SUB, LANE), [IN_VMEM], (part,))
        part = exchange(part, ("z",))
        return call(
            last_kernel, (payload, vmem(COUNT, SUB, LANE)), [IN_VMEM], (part,), out_specs=(IN_VMEM,) * 2
        )

    def gather(both):
        grads = call(stack_kernel, vmem(COUNT, 2 * SUB, LANE), [IN_VMEM], (both,))
        grads = exchange(grads, RING)
        return call(
            split_kernel, (payload, vmem(COUNT, SUB, LANE)), [IN_VMEM], (grads,), out_specs=(IN_VMEM,) * 2
        )

    with jax.named_scope("reduce_or_gather"):
        mine, kept = lax.cond(core == 0, reduce, gather, both)
        both = share(mine)
    with jax.named_scope("mix"):
        mixed = call(
            mix_kernel, vmem(COUNT, SUB, LANE), [IN_VMEM] * 5, (which, width, both, kept, slab)
        )
    with jax.named_scope("return_slab"):
        direction = untiles(exchange(mixed, RING), rows, cols)
    with jax.named_scope("adam"):
        block = jax.ShapeDtypeStruct((rows, cols), jnp.float32)
        outs = call(
            adam_kernel, (block,) * 4, [IN_VMEM] * 4,
            (particles[0], first_moment[0], second_moment[0], direction),
            out_specs=(ANYWHERE,) * 4,
            scratch=[vmem(rows, cols)] * 3 + [pltpu.SemaphoreType.DMA((1 + 3 * CHUNKS,))],
        )
    return tuple(out[None] for out in outs)


def solution(mesh):
    split = Mesh(mesh.devices.reshape(16, 4, 4, 2), ("z", "y", "x", "core"))
    block = P(("z", "y"), ("x", "core"), None)
    return jax.shard_map(
        body,
        mesh=split,
        in_specs=(block, block, block, block, P()),
        out_specs=(block, block, block, block),
        check_vma=False,
    )
```

```python
import math

import jax
import jax.numpy as jnp
from jax import lax
from jax.experimental import pallas as pl
from jax.experimental.pallas import tpu as pltpu
from jax.sharding import Mesh, PartitionSpec as P

ADAM_STEP = 10

beta_one = 0.9
beta_two = 0.999
learn_rate = 0.05
adam_eps = 1e-08

COUNT = 64
HALF = COUNT // 2
SUB, LANE = 8, 128
CHUNKS = 4
PACK = 16
PACKED = PACK // SUB

PLANE = ("y", "x")
RING = ("z", "y")


def dot(a, b, dims):
    return lax.dot_general(
        a, b, (dims, ((), ())),
        precision=lax.Precision.HIGHEST, preferred_element_type=jnp.float32,
    )


def iota(shape, dim):
    return lax.broadcasted_iota(jnp.int32, shape, dim)


def pack_kernel(width_ref, slab_ref, out_ref):
    x = jnp.concatenate([slab_ref[:, s, :] for s in range(SUB)], axis=1)
    gram = dot(x, jnp.concatenate([x, x], axis=0), ((1,), (1,)))
    lane = lax.rem(iota((COUNT, LANE), 1), COUNT)
    on_diag = jnp.where(lane == iota((COUNT, LANE), 0), gram, 0.0)
    norm_row = jnp.sum(on_diag, axis=0, keepdims=True)
    norm_col = 0.5 * jnp.sum(on_diag, axis=1, keepdims=True)
    dist = norm_col + norm_row - 2.0 * gram
    top = dist[:HALF]
    low = pltpu.roll(dist[HALF:], LANE - HALF, 1)
    lane = lax.rem(iota((HALF, LANE), 1), COUNT)
    keep = lane > iota((HALF, LANE), 0)
    both = jnp.where(keep, top, low)
    packed = jnp.where(iota((PACK, LANE), 1) < COUNT, both[:PACK], both[PACK:]) / width_ref[0:1]
    for k in range(PACKED):
        out_ref[k] = packed[k * SUB:(k + 1) * SUB]


def spread_kernel(both_ref, out_ref):
    total = both_ref[0] + both_ref[1]
    for k in range(out_ref.shape[0]):
        out_ref[k] = total


def stack_kernel(both_ref, out_ref):
    out_ref[:, 0:SUB, :] = both_ref[0]
    out_ref[:, SUB:, :] = both_ref[1]


def last_kernel(in_ref, out_ref, kept_ref):
    out_ref[0:PACKED] = jnp.sum(in_ref[...], axis=0)
    out_ref[PACKED:] = jnp.zeros((COUNT, SUB, LANE), jnp.float32)
    kept_ref[...] = jnp.zeros((COUNT, SUB, LANE), jnp.float32)


def split_kernel(in_ref, out_ref, kept_ref):
    out_ref[0:PACKED] = jnp.zeros((PACKED, SUB, LANE), jnp.float32)
    out_ref[PACKED:] = in_ref[:, 0:SUB, :]
    kept_ref[...] = in_ref[:, SUB:, :]


def sum_kernel(in_ref, out_ref):
    total = jnp.sum(in_ref[...], axis=0)
    for k in range(out_ref.shape[0]):
        out_ref[k] = total


def mix_kernel(core_ref, width_ref, both_ref, kept_ref, slab_ref, out_ref):
    packed = jnp.exp(-both_ref[0, 0:PACKED].reshape(PACK, LANE))
    both = jnp.concatenate([packed, pltpu.roll(packed, COUNT, 1)], axis=0)
    lane, row = iota((HALF, LANE), 1), iota((HALF, LANE), 0)
    top = jnp.where((lane > row) & (lane < COUNT), both, 0.0)
    low = jnp.where((lane >= HALF) & (lane - HALF < row), pltpu.roll(both, HALF, 1), 0.0)
    half = jnp.concatenate([top, low, jnp.zeros((LANE - COUNT, LANE), jnp.float32)], axis=0)
    eye = jnp.where(iota((LANE, LANE), 0) == iota((LANE, LANE), 1), 1.0, 0.0)
    kernel = (half + half.T + eye)[:COUNT, :COUNT]
    rowsum = jnp.sum(kernel, axis=1, keepdims=True)
    pull = 2.0 / width_ref[0:1, 0:1]
    own = pull * rowsum
    x = jnp.concatenate([slab_ref[:, s, :] for s in range(SUB)], axis=1)
    grads = jnp.where(core_ref[...] == 0.0, both_ref[1, PACKED:], kept_ref[...])
    g = jnp.concatenate([grads[:, s, :] for s in range(SUB)], axis=1)
    mixed = dot(kernel, g - pull * x, ((1,), (0,)))
    mixed = (mixed + own * x) * (1.0 / COUNT)
    for s in range(SUB):
        out_ref[:, s, :] = mixed[:, s * LANE:(s + 1) * LANE]


def adam_kernel(x_ref, m_ref, v_ref, d_ref, new_x, new_m, new_v, new_d, out_x, out_m, out_v, sems):
    copies = [pltpu.make_async_copy(d_ref, new_d, sems.at[0])]
    copies[0].start()
    rows = x_ref.shape[0] // CHUNKS
    for k in range(CHUNKS):
        part = pl.ds(k * rows, rows)
        direction = d_ref[part]
        first = beta_one * m_ref[part] + (1.0 - beta_one) * direction
        second = beta_two * v_ref[part] + (1.0 - beta_two) * direction * direction
        out_m[part] = first
        out_v[part] = second
        first_hat = first / (1.0 - beta_one**ADAM_STEP)
        second_hat = second / (1.0 - beta_two**ADAM_STEP)
        out_x[part] = x_ref[part] + learn_rate * first_hat / (jnp.sqrt(second_hat) + adam_eps)
        for i, (src, dst) in enumerate(((out_m, new_m), (out_v, new_v), (out_x, new_x))):
            copy = pltpu.make_async_copy(src.at[part], dst.at[part], sems.at[1 + 3 * k + i])
            copy.start()
            copies.append(copy)
    for copy in copies:
        copy.wait()


IN_VMEM = pl.BlockSpec(memory_space=pltpu.VMEM)
ANYWHERE = pl.BlockSpec(memory_space=pl.ANY)


def call(kernel, out_shape, in_specs, args, out_specs=IN_VMEM, scratch=()):
    args = [
        pltpu.with_memory_space_constraint(a, pltpu.VMEM if s is IN_VMEM else pltpu.HBM)
        for a, s in zip(args, in_specs)
    ]
    return pl.pallas_call(
        kernel, out_shape=out_shape, in_specs=in_specs, out_specs=out_specs, scratch_shapes=list(scratch)
    )(*args)


def vmem(*shape):
    return pltpu.VMEM(shape, jnp.float32)


def tiles(block):
    rows, cols = block.shape
    return (
        block.reshape(rows // SUB, SUB, cols // LANE, LANE)
        .transpose(0, 2, 1, 3)
        .reshape(-1, SUB, LANE)
    )


def untiles(parts, rows, cols):
    return (
        parts.reshape(rows // SUB, cols // LANE, SUB, LANE)
        .transpose(0, 2, 1, 3)
        .reshape(rows, cols)
    )


def exchange(array, axes):
    places = [0]
    for axis in sorted(axes, key="yxz".index):
        size = lax.axis_size(axis)
        step = math.prod(lax.axis_size(a) for a in axes[axes.index(axis) + 1:])
        places = [p + (i + size // 2) % size * step for p in places for i in range(size)]
    return lax.all_to_all(
        array, axes, split_axis=0, concat_axis=0, axis_index_groups=[places], tiled=True
    )


def share(array):
    return lax.all_gather(array, "core", axis=0, tiled=False)


def body(particles, gradients, first_moment, second_moment, spread):
    _, rows, cols = particles.shape
    entries = rows * cols * lax.axis_size("x") * lax.axis_size("core")
    plane = lax.axis_size("y") * lax.axis_size("x")
    depth = lax.axis_size("z")
    core = lax.axis_index("core")
    width = jnp.full((SUB, LANE), spread * entries, jnp.float32)
    which = jnp.full((1, SUB, LANE), core.astype(jnp.float32), jnp.float32)
    payload = vmem(PACKED + COUNT, SUB, LANE)
    with jax.named_scope("gather_slab"):
        grads = share(tiles(gradients[0]))
        slab = exchange(tiles(particles[0]), RING)
    with jax.named_scope("distances"):
        both = share(call(pack_kernel, vmem(PACKED, SUB, LANE), [IN_VMEM] * 2, (width, slab)))

    def reduce(both, grads):
        part = call(spread_kernel, vmem(plane, PACKED, SUB, LANE), [IN_VMEM], (both,))
        part = exchange(part, PLANE)
        part = call(sum_kernel, vmem(depth, PACKED, SUB, LANE), [IN_VMEM], (part,))
        part = exchange(part, ("z",))
        return call(
            last_kernel, (payload, vmem(COUNT, SUB, LANE)), [IN_VMEM], (part,), out_specs=(IN_VMEM,) * 2
        )

    def gather(both, grads):
        part = call(stack_kernel, vmem(COUNT, 2 * SUB, LANE), [IN_VMEM], (grads,))
        part = exchange(part, RING)
        return call(
            split_kernel, (payload, vmem(COUNT, SUB, LANE)), [IN_VMEM], (part,), out_specs=(IN_VMEM,) * 2
        )

    with jax.named_scope("reduce_or_gather"):
        mine, kept = lax.cond(core == 0, reduce, gather, both, grads)
        both = share(mine)
    with jax.named_scope("mix"):
        mixed = call(
            mix_kernel, vmem(COUNT, SUB, LANE), [IN_VMEM] * 5, (which, width, both, kept, slab)
        )
    with jax.named_scope("return_slab"):
        direction = untiles(exchange(mixed, RING), rows, cols)
    with jax.named_scope("adam"):
        block = jax.ShapeDtypeStruct((rows, cols), jnp.float32)
        outs = call(
            adam_kernel, (block,) * 4, [IN_VMEM] * 4,
            (particles[0], first_moment[0], second_moment[0], direction),
            out_specs=(ANYWHERE,) * 4,
            scratch=[vmem(rows, cols)] * 3 + [pltpu.SemaphoreType.DMA((1 + 3 * CHUNKS,))],
        )
    return tuple(out[None] for out in outs)


def solution(mesh):
    split = Mesh(mesh.devices.reshape(16, 4, 4, 2), ("z", "y", "x", "core"))
    block = P(("z", "y"), ("x", "core"), None)
    return jax.shard_map(
        body,
        mesh=split,
        in_specs=(block, block, block, block, P()),
        out_specs=(block, block, block, block),
        check_vma=False,
    )
```

```python
import math

import jax
import jax.numpy as jnp
from jax import lax
from jax.experimental import pallas as pl
from jax.experimental.pallas import tpu as pltpu
from jax.sharding import Mesh, PartitionSpec as P

ADAM_STEP = 10

beta_one = 0.9
beta_two = 0.999
learn_rate = 0.05
adam_eps = 1e-08

COUNT = 64
HALF = COUNT // 2
SUB, LANE = 8, 128
CHUNKS = 4
PACK = 16
PACKED = PACK // SUB

PLANE = ("y", "x")
RING = ("z", "y")


def dot(a, b, dims):
    return lax.dot_general(
        a, b, (dims, ((), ())),
        precision=lax.Precision.HIGHEST, preferred_element_type=jnp.float32,
    )


def thirds(a):
    high = a.astype(jnp.bfloat16)
    rest = a - high.astype(jnp.float32)
    mid = rest.astype(jnp.bfloat16)
    return high, mid, (rest - mid.astype(jnp.float32)).astype(jnp.bfloat16)


def product(a, b, dims):
    return lax.dot_general(a, b, (dims, ((), ())), preferred_element_type=jnp.float32)


def iota(shape, dim):
    return lax.broadcasted_iota(jnp.int32, shape, dim)


def pack_kernel(slab_ref, out_ref):
    x = jnp.concatenate([slab_ref[:, s, :] for s in range(2 * SUB)], axis=1)
    high, mid, low = thirds(x)
    parts = product(
        jnp.concatenate([high, mid, low], axis=0),
        jnp.concatenate([high, high, mid, mid, low, low], axis=0),
        ((1,), (1,)),
    )
    block = lambda i, j: parts[i * COUNT:(i + 1) * COUNT, j * LANE:(j + 1) * LANE]
    gram = block(1, 1) + (block(0, 2) + block(2, 0))
    gram = block(0, 0) + ((block(0, 1) + block(1, 0)) + gram)
    lane = lax.rem(iota((COUNT, LANE), 1), COUNT)
    on_diag = jnp.where(lane == iota((COUNT, LANE), 0), gram, 0.0)
    norm_row = jnp.sum(on_diag, axis=0, keepdims=True)
    norm_col = 0.5 * jnp.sum(on_diag, axis=1, keepdims=True)
    dist = norm_col + norm_row - 2.0 * gram
    top = dist[:HALF]
    low = pltpu.roll(dist[HALF:], LANE - HALF, 1)
    lane = lax.rem(iota((HALF, LANE), 1), COUNT)
    keep = lane > iota((HALF, LANE), 0)
    both = jnp.where(keep, top, low)
    packed = jnp.where(iota((PACK, LANE), 1) < COUNT, both[:PACK], both[PACK:])
    for i in range(out_ref.shape[0]):
        for k in range(PACKED):
            out_ref[i, k] = packed[k * SUB:(k + 1) * SUB]


def stack_kernel(first_ref, second_ref, out_ref):
    out_ref[:, 0:SUB, :] = first_ref[...]
    out_ref[:, SUB:, :] = second_ref[...]


def last_kernel(in_ref, slab_ref, out_ref, kept_ref):
    out_ref[0:PACKED] = jnp.sum(in_ref[...], axis=0)
    out_ref[PACKED:] = slab_ref[:, 0:SUB, :]
    kept_ref[...] = slab_ref[:, SUB:, :]


def turn_kernel(first_ref, second_ref, out_ref):
    depth = COUNT // 4
    for y in range(4):
        for z in range(depth):
            out_ref[z * 4 + y, 0:SUB, :] = first_ref[y * depth + z]
            out_ref[z * 4 + y, SUB:, :] = second_ref[y * depth + z]


def split_kernel(width_ref, slab_ref, out_ref, kept_ref):
    out_ref[0:PACKED] = jnp.broadcast_to(width_ref[...][None], (PACKED, SUB, LANE))
    depth = COUNT // 4
    for y in range(4):
        for z in range(depth):
            out_ref[PACKED + y * depth + z] = slab_ref[z * 4 + y, SUB:, :]
            kept_ref[y * depth + z] = slab_ref[z * 4 + y, 0:SUB, :]


def choose_kernel(x_ref, g_ref, send_ref, own_ref, sems):
    core = lax.axis_index("core")

    def fetch(send, own):
        copies = [
            pltpu.make_async_copy(send, send_ref, sems.at[0]),
            pltpu.make_async_copy(own, own_ref, sems.at[1]),
        ]
        for copy in copies:
            copy.start()
        for copy in copies:
            copy.wait()

    pl.when(core == 0)(lambda: fetch(x_ref, g_ref))
    pl.when(core != 0)(lambda: fetch(g_ref, x_ref))


def sum_kernel(in_ref, out_ref):
    total = jnp.sum(in_ref[...], axis=0)
    for k in range(out_ref.shape[0]):
        out_ref[k] = total


def mix_kernel(core_ref, both_ref, kept_ref, out_ref):
    width = both_ref[0, 0][0:1]
    packed = jnp.exp(-both_ref[1, 0:PACKED].reshape(PACK, LANE) / width)
    both = jnp.concatenate([packed, pltpu.roll(packed, COUNT, 1)], axis=0)
    lane, row = iota((HALF, LANE), 1), iota((HALF, LANE), 0)
    top = jnp.where((lane > row) & (lane < COUNT), both, 0.0)
    low = jnp.where((lane >= HALF) & (lane - HALF < row), pltpu.roll(both, HALF, 1), 0.0)
    half = jnp.concatenate([top, low, jnp.zeros((LANE - COUNT, LANE), jnp.float32)], axis=0)
    eye = jnp.where(iota((LANE, LANE), 0) == iota((LANE, LANE), 1), 1.0, 0.0)
    kernel = (half + half.T + eye)[:COUNT, :COUNT]
    rowsum = jnp.sum(kernel, axis=1, keepdims=True)
    pull = 2.0 / width[:, 0:1]
    own = pull * rowsum
    second = core_ref[...] == 1.0
    parts = jnp.where(second, kept_ref[...], both_ref[1, PACKED:])
    grads = jnp.where(second, both_ref[0, PACKED:], kept_ref[...])
    x = jnp.concatenate([parts[:, s, :] for s in range(SUB)], axis=1)
    g = jnp.concatenate([grads[:, s, :] for s in range(SUB)], axis=1)
    mixed = dot(kernel, g - pull * x, ((1,), (0,)))
    mixed = (mixed + own * x) * (1.0 / COUNT)
    for s in range(SUB):
        out_ref[:, s, :] = mixed[:, s * LANE:(s + 1) * LANE]


def adam_kernel(x_ref, m_ref, v_ref, d_ref, new_x, new_m, new_v, new_d, out_x, out_m, out_v, sems):
    copies = [pltpu.make_async_copy(d_ref, new_d, sems.at[0])]
    copies[0].start()
    rows = x_ref.shape[0] // CHUNKS
    for k in range(CHUNKS):
        part = pl.ds(k * rows, rows)
        direction = d_ref[part]
        first = beta_one * m_ref[part] + (1.0 - beta_one) * direction
        second = beta_two * v_ref[part] + (1.0 - beta_two) * direction * direction
        out_m[part] = first
        out_v[part] = second
        first_hat = first / (1.0 - beta_one**ADAM_STEP)
        second_hat = second / (1.0 - beta_two**ADAM_STEP)
        out_x[part] = x_ref[part] + learn_rate * first_hat / (jnp.sqrt(second_hat) + adam_eps)
        for i, (src, dst) in enumerate(((out_m, new_m), (out_v, new_v), (out_x, new_x))):
            copy = pltpu.make_async_copy(src.at[part], dst.at[part], sems.at[1 + 3 * k + i])
            copy.start()
            copies.append(copy)
    for copy in copies:
        copy.wait()


IN_VMEM = pl.BlockSpec(memory_space=pltpu.VMEM)
ANYWHERE = pl.BlockSpec(memory_space=pl.ANY)


def call(kernel, out_shape, in_specs, args, out_specs=IN_VMEM, scratch=()):
    args = [
        pltpu.with_memory_space_constraint(a, pltpu.VMEM if s is IN_VMEM else pltpu.HBM)
        for a, s in zip(args, in_specs)
    ]
    return pl.pallas_call(
        kernel, out_shape=out_shape, in_specs=in_specs, out_specs=out_specs, scratch_shapes=list(scratch)
    )(*args)


def vmem(*shape):
    return pltpu.VMEM(shape, jnp.float32)


def tiles(block):
    rows, cols = block.shape
    return (
        block.reshape(rows // SUB, SUB, cols // LANE, LANE)
        .transpose(0, 2, 1, 3)
        .reshape(-1, SUB, LANE)
    )


def untiles(parts, rows, cols):
    return (
        parts.reshape(rows // SUB, cols // LANE, SUB, LANE)
        .transpose(0, 2, 1, 3)
        .reshape(rows, cols)
    )


def exchange(array, axes):
    places = [0]
    for axis in sorted(axes, key="yxz".index):
        size = lax.axis_size(axis)
        step = math.prod(lax.axis_size(a) for a in axes[axes.index(axis) + 1:])
        places = [p + (i + size // 2) % size * step for p in places for i in range(size)]
    return lax.all_to_all(
        array, axes, split_axis=0, concat_axis=0, axis_index_groups=[places], tiled=True
    )


def share(array):
    return lax.all_gather(array, "core", axis=0, tiled=False)


def body(particles, gradients, first_moment, second_moment, spread):
    _, rows, cols = particles.shape
    entries = rows * cols * lax.axis_size("x") * lax.axis_size("core")
    plane = lax.axis_size("y") * lax.axis_size("x")
    depth = lax.axis_size("z")
    core = lax.axis_index("core")
    which = jnp.full((1, SUB, LANE), core.astype(jnp.float32), jnp.float32)
    payload = vmem(PACKED + COUNT, SUB, LANE)
    with jax.named_scope("swap"):
        x, g = tiles(particles[0]), tiles(gradients[0])
        send, own = call(
            choose_kernel, (vmem(COUNT, SUB, LANE),) * 2, [ANYWHERE] * 2, (x, g), out_specs=(IN_VMEM,) * 2,
            scratch=[pltpu.SemaphoreType.DMA((2,))],
        )
        others = share(send)

    def reduce(own, others, spread):
        slab = call(stack_kernel, vmem(COUNT, 2 * SUB, LANE), [IN_VMEM] * 2, (others[0], own))
        slab = exchange(slab, RING)
        part = call(pack_kernel, vmem(plane, PACKED, SUB, LANE), [IN_VMEM], (slab,))
        part = exchange(part, PLANE)
        part = call(sum_kernel, vmem(depth, PACKED, SUB, LANE), [IN_VMEM], (part,))
        part = exchange(part, ("z",))
        return call(
            last_kernel, (payload, vmem(COUNT, SUB, LANE)), [IN_VMEM] * 2, (part, slab), out_specs=(IN_VMEM,) * 2
        )

    def gather(own, others, spread):
        first = exchange(own, ("y",))
        second = exchange(others[1], ("y",))
        slab = call(turn_kernel, vmem(COUNT, 2 * SUB, LANE), [IN_VMEM] * 2, (first, second))
        slab = exchange(slab, ("z",))
        width = jnp.full((SUB, LANE), spread * entries, jnp.float32)
        return call(
            split_kernel, (payload, vmem(COUNT, SUB, LANE)), [IN_VMEM] * 2, (width, slab),
            out_specs=(IN_VMEM,) * 2
        )

    with jax.named_scope("reduce_or_gather"):
        mine, kept = lax.cond(core == 1, reduce, gather, own, others, spread)
        both = share(mine)
    with jax.named_scope("mix"):
        mixed = call(
            mix_kernel, vmem(COUNT, SUB, LANE), [IN_VMEM] * 3, (which, both, kept)
        )
    with jax.named_scope("return_slab"):
        direction = untiles(exchange(mixed, RING), rows, cols)
    with jax.named_scope("adam"):
        block = jax.ShapeDtypeStruct((rows, cols), jnp.float32)
        outs = call(
            adam_kernel, (block,) * 4, [IN_VMEM] * 4,
            (particles[0], first_moment[0], second_moment[0], direction),
            out_specs=(ANYWHERE,) * 4,
            scratch=[vmem(rows, cols)] * 3 + [pltpu.SemaphoreType.DMA((1 + 3 * CHUNKS,))],
        )
    return tuple(out[None] for out in outs)


def solution(mesh):
    split = Mesh(mesh.devices.reshape(16, 4, 4, 2), ("z", "y", "x", "core"))
    block = P(("z", "y"), ("x", "core"), None)
    return jax.shard_map(
        body,
        mesh=split,
        in_specs=(block, block, block, block, P()),
        out_specs=(block, block, block, block),
        check_vma=False,
    )
```

```python
import math

import jax
import jax.numpy as jnp
from jax import lax
from jax.experimental import pallas as pl
from jax.experimental.pallas import tpu as pltpu
from jax.sharding import Mesh, PartitionSpec as P

ADAM_STEP = 10

beta_one = 0.9
beta_two = 0.999
learn_rate = 0.05
adam_eps = 1e-08

COUNT = 64
HALF = COUNT // 2
SUB, LANE = 8, 128
CHUNKS = 4
PACK = 16
PACKED = PACK // SUB

PLANE = ("y", "x")
RING = ("z", "y")


def dot(a, b, dims):
    return lax.dot_general(
        a, b, (dims, ((), ())),
        precision=lax.Precision.HIGHEST, preferred_element_type=jnp.float32,
    )


def iota(shape, dim):
    return lax.broadcasted_iota(jnp.int32, shape, dim)


def pack_kernel(slab_ref, out_ref):
    x = jnp.concatenate([slab_ref[:, s, :] for s in range(2 * SUB)], axis=1)
    gram = dot(x, jnp.concatenate([x, x], axis=0), ((1,), (1,)))
    lane = lax.rem(iota((COUNT, LANE), 1), COUNT)
    on_diag = jnp.where(lane == iota((COUNT, LANE), 0), gram, 0.0)
    norm_row = jnp.sum(on_diag, axis=0, keepdims=True)
    norm_col = 0.5 * jnp.sum(on_diag, axis=1, keepdims=True)
    dist = norm_col + norm_row - 2.0 * gram
    top = dist[:HALF]
    low = pltpu.roll(dist[HALF:], LANE - HALF, 1)
    lane = lax.rem(iota((HALF, LANE), 1), COUNT)
    keep = lane > iota((HALF, LANE), 0)
    both = jnp.where(keep, top, low)
    packed = jnp.where(iota((PACK, LANE), 1) < COUNT, both[:PACK], both[PACK:])
    for i in range(out_ref.shape[0]):
        for k in range(PACKED):
            out_ref[i, k] = packed[k * SUB:(k + 1) * SUB]


def stack_kernel(first_ref, second_ref, out_ref):
    out_ref[:, 0:SUB, :] = first_ref[...]
    out_ref[:, SUB:, :] = second_ref[...]


def last_kernel(in_ref, slab_ref, out_ref, kept_ref):
    out_ref[0:PACKED] = jnp.sum(in_ref[...], axis=0)
    out_ref[PACKED:] = slab_ref[:, 0:SUB, :]
    kept_ref[...] = slab_ref[:, SUB:, :]


def turn_kernel(first_ref, second_ref, out_ref):
    depth = COUNT // 4
    for y in range(4):
        for z in range(depth):
            out_ref[z * 4 + y, 0:SUB, :] = first_ref[y * depth + z]
            out_ref[z * 4 + y, SUB:, :] = second_ref[y * depth + z]


def split_kernel(width_ref, slab_ref, out_ref, kept_ref):
    out_ref[0:PACKED] = jnp.broadcast_to(width_ref[...][None], (PACKED, SUB, LANE))
    depth = COUNT // 4
    for y in range(4):
        for z in range(depth):
            out_ref[PACKED + y * depth + z] = slab_ref[z * 4 + y, SUB:, :]
            kept_ref[y * depth + z] = slab_ref[z * 4 + y, 0:SUB, :]


def choose_kernel(x_ref, g_ref, send_ref, own_ref, sems):
    core = lax.axis_index("core")

    def fetch(send, own):
        copies = [
            pltpu.make_async_copy(send, send_ref, sems.at[0]),
            pltpu.make_async_copy(own, own_ref, sems.at[1]),
        ]
        for copy in copies:
            copy.start()
        for copy in copies:
            copy.wait()

    pl.when(core == 0)(lambda: fetch(x_ref, g_ref))
    pl.when(core != 0)(lambda: fetch(g_ref, x_ref))


def sum_kernel(in_ref, out_ref):
    total = jnp.sum(in_ref[...], axis=0)
    for k in range(out_ref.shape[0]):
        out_ref[k] = total


def mix_kernel(core_ref, both_ref, kept_ref, out_ref):
    width = both_ref[0, 0][0:1]
    packed = jnp.exp(-both_ref[1, 0:PACKED].reshape(PACK, LANE) / width)
    both = jnp.concatenate([packed, pltpu.roll(packed, COUNT, 1)], axis=0)
    lane, row = iota((HALF, LANE), 1), iota((HALF, LANE), 0)
    top = jnp.where((lane > row) & (lane < COUNT), both, 0.0)
    low = jnp.where((lane >= HALF) & (lane - HALF < row), pltpu.roll(both, HALF, 1), 0.0)
    half = jnp.concatenate([top, low, jnp.zeros((LANE - COUNT, LANE), jnp.float32)], axis=0)
    eye = jnp.where(iota((LANE, LANE), 0) == iota((LANE, LANE), 1), 1.0, 0.0)
    kernel = (half + half.T + eye)[:COUNT, :COUNT]
    rowsum = jnp.sum(kernel, axis=1, keepdims=True)
    pull = 2.0 / width[:, 0:1]
    own = pull * rowsum
    second = core_ref[...] == 1.0
    parts = jnp.where(second, kept_ref[...], both_ref[1, PACKED:])
    grads = jnp.where(second, both_ref[0, PACKED:], kept_ref[...])
    x = jnp.concatenate([parts[:, s, :] for s in range(SUB)], axis=1)
    g = jnp.concatenate([grads[:, s, :] for s in range(SUB)], axis=1)
    mixed = dot(kernel, g - pull * x, ((1,), (0,)))
    mixed = (mixed + own * x) * (1.0 / COUNT)
    for s in range(SUB):
        out_ref[:, s, :] = mixed[:, s * LANE:(s + 1) * LANE]


def adam_kernel(x_ref, m_ref, v_ref, d_ref, new_x, new_m, new_v, new_d, out_x, out_m, out_v, sems):
    copies = [pltpu.make_async_copy(d_ref, new_d, sems.at[0])]
    copies[0].start()
    rows = x_ref.shape[0] // CHUNKS
    for k in range(CHUNKS):
        part = pl.ds(k * rows, rows)
        direction = d_ref[part]
        first = beta_one * m_ref[part] + (1.0 - beta_one) * direction
        second = beta_two * v_ref[part] + (1.0 - beta_two) * direction * direction
        out_m[part] = first
        out_v[part] = second
        first_hat = first / (1.0 - beta_one**ADAM_STEP)
        second_hat = second / (1.0 - beta_two**ADAM_STEP)
        out_x[part] = x_ref[part] + learn_rate * first_hat / (jnp.sqrt(second_hat) + adam_eps)
        for i, (src, dst) in enumerate(((out_m, new_m), (out_v, new_v), (out_x, new_x))):
            copy = pltpu.make_async_copy(src.at[part], dst.at[part], sems.at[1 + 3 * k + i])
            copy.start()
            copies.append(copy)
    for copy in copies:
        copy.wait()


IN_VMEM = pl.BlockSpec(memory_space=pltpu.VMEM)
ANYWHERE = pl.BlockSpec(memory_space=pl.ANY)


def call(kernel, out_shape, in_specs, args, out_specs=IN_VMEM, scratch=()):
    args = [
        pltpu.with_memory_space_constraint(a, pltpu.VMEM if s is IN_VMEM else pltpu.HBM)
        for a, s in zip(args, in_specs)
    ]
    return pl.pallas_call(
        kernel, out_shape=out_shape, in_specs=in_specs, out_specs=out_specs, scratch_shapes=list(scratch)
    )(*args)


def vmem(*shape):
    return pltpu.VMEM(shape, jnp.float32)


def tiles(block):
    rows, cols = block.shape
    return (
        block.reshape(rows // SUB, SUB, cols // LANE, LANE)
        .transpose(0, 2, 1, 3)
        .reshape(-1, SUB, LANE)
    )


def untiles(parts, rows, cols):
    return (
        parts.reshape(rows // SUB, cols // LANE, SUB, LANE)
        .transpose(0, 2, 1, 3)
        .reshape(rows, cols)
    )


def exchange(array, axes):
    places = [0]
    for axis in sorted(axes, key="yxz".index):
        size = lax.axis_size(axis)
        step = math.prod(lax.axis_size(a) for a in axes[axes.index(axis) + 1:])
        places = [p + (i + size // 2) % size * step for p in places for i in range(size)]
    return lax.all_to_all(
        array, axes, split_axis=0, concat_axis=0, axis_index_groups=[places], tiled=True
    )


def share(array):
    return lax.all_gather(array, "core", axis=0, tiled=False)


def body(particles, gradients, first_moment, second_moment, spread):
    _, rows, cols = particles.shape
    entries = rows * cols * lax.axis_size("x") * lax.axis_size("core")
    plane = lax.axis_size("y") * lax.axis_size("x")
    depth = lax.axis_size("z")
    core = lax.axis_index("core")
    which = jnp.full((1, SUB, LANE), core.astype(jnp.float32), jnp.float32)
    payload = vmem(PACKED + COUNT, SUB, LANE)
    with jax.named_scope("swap"):
        x, g = tiles(particles[0]), tiles(gradients[0])
        send, own = call(
            choose_kernel, (vmem(COUNT, SUB, LANE),) * 2, [ANYWHERE] * 2, (x, g), out_specs=(IN_VMEM,) * 2,
            scratch=[pltpu.SemaphoreType.DMA((2,))],
        )
        others = share(send)

    def reduce(own, others, spread):
        slab = call(stack_kernel, vmem(COUNT, 2 * SUB, LANE), [IN_VMEM] * 2, (others[0], own))
        slab = exchange(slab, RING)
        part = call(pack_kernel, vmem(plane, PACKED, SUB, LANE), [IN_VMEM], (slab,))
        part = exchange(part, PLANE)
        part = call(sum_kernel, vmem(depth, PACKED, SUB, LANE), [IN_VMEM], (part,))
        part = exchange(part, ("z",))
        return call(
            last_kernel, (payload, vmem(COUNT, SUB, LANE)), [IN_VMEM] * 2, (part, slab), out_specs=(IN_VMEM,) * 2
        )

    def gather(own, others, spread):
        first = exchange(own, ("y",))
        second = exchange(others[1], ("y",))
        slab = call(turn_kernel, vmem(COUNT, 2 * SUB, LANE), [IN_VMEM] * 2, (first, second))
        slab = exchange(slab, ("z",))
        width = jnp.full((SUB, LANE), spread * entries, jnp.float32)
        return call(
            split_kernel, (payload, vmem(COUNT, SUB, LANE)), [IN_VMEM] * 2, (width, slab),
            out_specs=(IN_VMEM,) * 2
        )

    with jax.named_scope("reduce_or_gather"):
        mine, kept = lax.cond(core == 1, reduce, gather, own, others, spread)
        both = share(mine)
    with jax.named_scope("mix"):
        mixed = call(
            mix_kernel, vmem(COUNT, SUB, LANE), [IN_VMEM] * 3, (which, both, kept)
        )
    with jax.named_scope("return_slab"):
        direction = untiles(exchange(mixed, RING), rows, cols)
    with jax.named_scope("adam"):
        block = jax.ShapeDtypeStruct((rows, cols), jnp.float32)
        outs = call(
            adam_kernel, (block,) * 4, [IN_VMEM] * 4,
            (particles[0], first_moment[0], second_moment[0], direction),
            out_specs=(ANYWHERE,) * 4,
            scratch=[vmem(rows, cols)] * 3 + [pltpu.SemaphoreType.DMA((1 + 3 * CHUNKS,))],
        )
    return tuple(out[None] for out in outs)


def solution(mesh):
    split = Mesh(mesh.devices.reshape(16, 4, 4, 2), ("z", "y", "x", "core"))
    block = P(("z", "y"), ("x", "core"), None)
    return jax.shard_map(
        body,
        mesh=split,
        in_specs=(block, block, block, block, P()),
        out_specs=(block, block, block, block),
        check_vma=False,
    )
```

```python
import math

import jax
import jax.numpy as jnp
from jax import lax
from jax.experimental import pallas as pl
from jax.experimental.pallas import tpu as pltpu
from jax.sharding import Mesh, PartitionSpec as P

ADAM_STEP = 10

beta_one = 0.9
beta_two = 0.999
learn_rate = 0.05
adam_eps = 1e-08

COUNT = 64
HALF = COUNT // 2
SUB, LANE = 8, 128
CHUNKS = 4
PACK = 16
PACKED = PACK // SUB

PLANE = ("y", "x")
RING = ("z", "y")


def dot(a, b, dims):
    return lax.dot_general(
        a, b, (dims, ((), ())),
        precision=lax.Precision.HIGHEST, preferred_element_type=jnp.float32,
    )


def iota(shape, dim):
    return lax.broadcasted_iota(jnp.int32, shape, dim)


def pack_kernel(slab_ref, out_ref):
    x = jnp.concatenate([slab_ref[:, s, :] for s in range(2 * SUB)], axis=1)
    gram = dot(x, x, ((1,), (1,)))
    gram = jnp.concatenate([gram, gram], axis=1)
    lane = lax.rem(iota((COUNT, LANE), 1), COUNT)
    on_diag = jnp.where(lane == iota((COUNT, LANE), 0), gram, 0.0)
    norm_row = jnp.sum(on_diag, axis=0, keepdims=True)
    norm_col = 0.5 * jnp.sum(on_diag, axis=1, keepdims=True)
    dist = norm_col + norm_row - 2.0 * gram
    top = dist[:HALF]
    low = pltpu.roll(dist[HALF:], LANE - HALF, 1)
    lane = lax.rem(iota((HALF, LANE), 1), COUNT)
    keep = lane > iota((HALF, LANE), 0)
    both = jnp.where(keep, top, low)
    packed = jnp.where(iota((PACK, LANE), 1) < COUNT, both[:PACK], both[PACK:])
    for i in range(out_ref.shape[0]):
        for k in range(PACKED):
            out_ref[i, k] = packed[k * SUB:(k + 1) * SUB]


def stack_kernel(first_ref, second_ref, out_ref):
    out_ref[:, 0:SUB, :] = first_ref[...]
    out_ref[:, SUB:, :] = second_ref[...]


def last_kernel(in_ref, slab_ref, out_ref, kept_ref):
    out_ref[0:PACKED] = jnp.sum(in_ref[...], axis=0)
    out_ref[PACKED:] = slab_ref[:, 0:SUB, :]
    kept_ref[...] = slab_ref[:, SUB:, :]


def turn_kernel(first_ref, second_ref, out_ref):
    depth = COUNT // 4
    for y in range(4):
        for z in range(depth):
            out_ref[z * 4 + y, 0:SUB, :] = first_ref[y * depth + z]
            out_ref[z * 4 + y, SUB:, :] = second_ref[y * depth + z]


def split_kernel(width_ref, slab_ref, out_ref, kept_ref):
    out_ref[0:PACKED] = jnp.broadcast_to(width_ref[...][None], (PACKED, SUB, LANE))
    depth = COUNT // 4
    for y in range(4):
        for z in range(depth):
            out_ref[PACKED + y * depth + z] = slab_ref[z * 4 + y, SUB:, :]
            kept_ref[y * depth + z] = slab_ref[z * 4 + y, 0:SUB, :]


def choose_kernel(x_ref, g_ref, send_ref, own_ref, sems):
    core = lax.axis_index("core")

    def fetch(send, own):
        copies = [
            pltpu.make_async_copy(send, send_ref, sems.at[0]),
            pltpu.make_async_copy(own, own_ref, sems.at[1]),
        ]
        for copy in copies:
            copy.start()
        for copy in copies:
            copy.wait()

    pl.when(core == 0)(lambda: fetch(x_ref, g_ref))
    pl.when(core != 0)(lambda: fetch(g_ref, x_ref))


def sum_kernel(in_ref, out_ref):
    total = jnp.sum(in_ref[...], axis=0)
    for k in range(out_ref.shape[0]):
        out_ref[k] = total


def mix_kernel(core_ref, both_ref, kept_ref, out_ref):
    width = both_ref[0, 0][0:1]
    packed = jnp.exp(-both_ref[1, 0:PACKED].reshape(PACK, LANE) / width)
    both = jnp.concatenate([packed, pltpu.roll(packed, COUNT, 1)], axis=0)
    lane, row = iota((HALF, LANE), 1), iota((HALF, LANE), 0)
    top = jnp.where((lane > row) & (lane < COUNT), both, 0.0)
    low = jnp.where((lane >= HALF) & (lane - HALF < row), pltpu.roll(both, HALF, 1), 0.0)
    half = jnp.concatenate([top, low, jnp.zeros((LANE - COUNT, LANE), jnp.float32)], axis=0)
    eye = jnp.where(iota((LANE, LANE), 0) == iota((LANE, LANE), 1), 1.0, 0.0)
    kernel = (half + half.T + eye)[:COUNT, :COUNT]
    rowsum = jnp.sum(kernel, axis=1, keepdims=True)
    pull = 2.0 / width[:, 0:1]
    own = pull * rowsum
    second = core_ref[...] == 1.0
    parts = jnp.where(second, kept_ref[...], both_ref[1, PACKED:])
    grads = jnp.where(second, both_ref[0, PACKED:], kept_ref[...])
    x = jnp.concatenate([parts[:, s, :] for s in range(SUB)], axis=1)
    g = jnp.concatenate([grads[:, s, :] for s in range(SUB)], axis=1)
    mixed = dot(kernel, g - pull * x, ((1,), (0,)))
    mixed = (mixed + own * x) * (1.0 / COUNT)
    for s in range(SUB):
        out_ref[:, s, :] = mixed[:, s * LANE:(s + 1) * LANE]


def adam_kernel(x_ref, m_ref, v_ref, d_ref, new_x, new_m, new_v, new_d, out_x, out_m, out_v, sems):
    copies = [pltpu.make_async_copy(d_ref, new_d, sems.at[0])]
    copies[0].start()
    rows = x_ref.shape[0] // CHUNKS
    for k in range(CHUNKS):
        part = pl.ds(k * rows, rows)
        direction = d_ref[part]
        first = beta_one * m_ref[part] + (1.0 - beta_one) * direction
        second = beta_two * v_ref[part] + (1.0 - beta_two) * direction * direction
        out_m[part] = first
        out_v[part] = second
        first_hat = first / (1.0 - beta_one**ADAM_STEP)
        second_hat = second / (1.0 - beta_two**ADAM_STEP)
        out_x[part] = x_ref[part] + learn_rate * first_hat / (jnp.sqrt(second_hat) + adam_eps)
        for i, (src, dst) in enumerate(((out_m, new_m), (out_v, new_v), (out_x, new_x))):
            copy = pltpu.make_async_copy(src.at[part], dst.at[part], sems.at[1 + 3 * k + i])
            copy.start()
            copies.append(copy)
    for copy in copies:
        copy.wait()


IN_VMEM = pl.BlockSpec(memory_space=pltpu.VMEM)
ANYWHERE = pl.BlockSpec(memory_space=pl.ANY)


def call(kernel, out_shape, in_specs, args, out_specs=IN_VMEM, scratch=()):
    args = [
        pltpu.with_memory_space_constraint(a, pltpu.VMEM if s is IN_VMEM else pltpu.HBM)
        for a, s in zip(args, in_specs)
    ]
    return pl.pallas_call(
        kernel, out_shape=out_shape, in_specs=in_specs, out_specs=out_specs, scratch_shapes=list(scratch)
    )(*args)


def vmem(*shape):
    return pltpu.VMEM(shape, jnp.float32)


def tiles(block):
    rows, cols = block.shape
    return (
        block.reshape(rows // SUB, SUB, cols // LANE, LANE)
        .transpose(0, 2, 1, 3)
        .reshape(-1, SUB, LANE)
    )


def untiles(parts, rows, cols):
    return (
        parts.reshape(rows // SUB, cols // LANE, SUB, LANE)
        .transpose(0, 2, 1, 3)
        .reshape(rows, cols)
    )


def exchange(array, axes):
    places = [0]
    for axis in sorted(axes, key="yxz".index):
        size = lax.axis_size(axis)
        step = math.prod(lax.axis_size(a) for a in axes[axes.index(axis) + 1:])
        places = [p + (i + size // 2) % size * step for p in places for i in range(size)]
    return lax.all_to_all(
        array, axes, split_axis=0, concat_axis=0, axis_index_groups=[places], tiled=True
    )


def share(array):
    return lax.all_gather(array, "core", axis=0, tiled=False)


def body(particles, gradients, first_moment, second_moment, spread):
    _, rows, cols = particles.shape
    entries = rows * cols * lax.axis_size("x") * lax.axis_size("core")
    plane = lax.axis_size("y") * lax.axis_size("x")
    depth = lax.axis_size("z")
    core = lax.axis_index("core")
    which = jnp.full((1, SUB, LANE), core.astype(jnp.float32), jnp.float32)
    payload = vmem(PACKED + COUNT, SUB, LANE)
    with jax.named_scope("swap"):
        x, g = tiles(particles[0]), tiles(gradients[0])
        send, own = call(
            choose_kernel, (vmem(COUNT, SUB, LANE),) * 2, [ANYWHERE] * 2, (x, g), out_specs=(IN_VMEM,) * 2,
            scratch=[pltpu.SemaphoreType.DMA((2,))],
        )
        others = share(send)

    def reduce(own, others, spread):
        slab = call(stack_kernel, vmem(COUNT, 2 * SUB, LANE), [IN_VMEM] * 2, (others[0], own))
        slab = exchange(slab, RING)
        part = call(pack_kernel, vmem(plane, PACKED, SUB, LANE), [IN_VMEM], (slab,))
        part = exchange(part, PLANE)
        part = call(sum_kernel, vmem(depth, PACKED, SUB, LANE), [IN_VMEM], (part,))
        part = exchange(part, ("z",))
        return call(
            last_kernel, (payload, vmem(COUNT, SUB, LANE)), [IN_VMEM] * 2, (part, slab), out_specs=(IN_VMEM,) * 2
        )

    def gather(own, others, spread):
        first = exchange(own, ("y",))
        second = exchange(others[1], ("y",))
        slab = call(turn_kernel, vmem(COUNT, 2 * SUB, LANE), [IN_VMEM] * 2, (first, second))
        slab = exchange(slab, ("z",))
        width = jnp.full((SUB, LANE), spread * entries, jnp.float32)
        return call(
            split_kernel, (payload, vmem(COUNT, SUB, LANE)), [IN_VMEM] * 2, (width, slab),
            out_specs=(IN_VMEM,) * 2
        )

    with jax.named_scope("reduce_or_gather"):
        mine, kept = lax.cond(core == 1, reduce, gather, own, others, spread)
        both = share(mine)
    with jax.named_scope("mix"):
        mixed = call(
            mix_kernel, vmem(COUNT, SUB, LANE), [IN_VMEM] * 3, (which, both, kept)
        )
    with jax.named_scope("return_slab"):
        direction = untiles(exchange(mixed, RING), rows, cols)
    with jax.named_scope("adam"):
        block = jax.ShapeDtypeStruct((rows, cols), jnp.float32)
        outs = call(
            adam_kernel, (block,) * 4, [IN_VMEM] * 4,
            (particles[0], first_moment[0], second_moment[0], direction),
            out_specs=(ANYWHERE,) * 4,
            scratch=[vmem(rows, cols)] * 3 + [pltpu.SemaphoreType.DMA((1 + 3 * CHUNKS,))],
        )
    return tuple(out[None] for out in outs)


def solution(mesh):
    split = Mesh(mesh.devices.reshape(16, 4, 4, 2), ("z", "y", "x", "core"))
    block = P(("z", "y"), ("x", "core"), None)
    return jax.shard_map(
        body,
        mesh=split,
        in_specs=(block, block, block, block, P()),
        out_specs=(block, block, block, block),
        check_vma=False,
    )
```

```python
import math

import jax
import jax.numpy as jnp
from jax import lax
from jax.experimental import pallas as pl
from jax.experimental.pallas import tpu as pltpu
from jax.sharding import Mesh, PartitionSpec as P

ADAM_STEP = 10

beta_one = 0.9
beta_two = 0.999
learn_rate = 0.05
adam_eps = 1e-08

COUNT = 64
HALF = COUNT // 2
SUB, LANE = 8, 128
CHUNKS = 2
PACK = 16
PACKED = PACK // SUB

PLANE = ("y", "x")
RING = ("z", "y")


def dot(a, b, dims):
    return lax.dot_general(
        a, b, (dims, ((), ())),
        precision=lax.Precision.HIGHEST, preferred_element_type=jnp.float32,
    )


def iota(shape, dim):
    return lax.broadcasted_iota(jnp.int32, shape, dim)


def pack_kernel(slab_ref, out_ref):
    x = jnp.concatenate([slab_ref[:, s, :] for s in range(2 * SUB)], axis=1)
    gram = dot(x, x, ((1,), (1,)))
    gram = jnp.concatenate([gram, gram], axis=1)
    lane = lax.rem(iota((COUNT, LANE), 1), COUNT)
    on_diag = jnp.where(lane == iota((COUNT, LANE), 0), gram, 0.0)
    norm_row = jnp.sum(on_diag, axis=0, keepdims=True)
    norm_col = 0.5 * jnp.sum(on_diag, axis=1, keepdims=True)
    dist = norm_col + norm_row - 2.0 * gram
    top = dist[:HALF]
    low = pltpu.roll(dist[HALF:], LANE - HALF, 1)
    lane = lax.rem(iota((HALF, LANE), 1), COUNT)
    keep = lane > iota((HALF, LANE), 0)
    both = jnp.where(keep, top, low)
    packed = jnp.where(iota((PACK, LANE), 1) < COUNT, both[:PACK], both[PACK:])
    for i in range(out_ref.shape[0]):
        for k in range(PACKED):
            out_ref[i, k] = packed[k * SUB:(k + 1) * SUB]


def stack_kernel(first_ref, second_ref, out_ref):
    out_ref[:, 0:SUB, :] = first_ref[...]
    out_ref[:, SUB:, :] = second_ref[...]


def last_kernel(in_ref, slab_ref, out_ref, kept_ref):
    out_ref[0:PACKED] = jnp.sum(in_ref[...], axis=0)
    out_ref[PACKED:] = slab_ref[:, 0:SUB, :]
    kept_ref[...] = slab_ref[:, SUB:, :]


def turn_kernel(first_ref, second_ref, out_ref):
    depth = COUNT // 4
    for y in range(4):
        for z in range(depth):
            out_ref[z * 4 + y, 0:SUB, :] = first_ref[y * depth + z]
            out_ref[z * 4 + y, SUB:, :] = second_ref[y * depth + z]


def split_kernel(width_ref, slab_ref, out_ref, kept_ref):
    out_ref[0:PACKED] = jnp.broadcast_to(width_ref[...][None], (PACKED, SUB, LANE))
    depth = COUNT // 4
    for y in range(4):
        for z in range(depth):
            out_ref[PACKED + y * depth + z] = slab_ref[z * 4 + y, SUB:, :]
            kept_ref[y * depth + z] = slab_ref[z * 4 + y, 0:SUB, :]


def choose_kernel(x_ref, g_ref, send_ref, own_ref, sems):
    core = lax.axis_index("core")

    def fetch(send, own):
        copies = [
            pltpu.make_async_copy(send, send_ref, sems.at[0]),
            pltpu.make_async_copy(own, own_ref, sems.at[1]),
        ]
        for copy in copies:
            copy.start()
        for copy in copies:
            copy.wait()

    pl.when(core == 0)(lambda: fetch(x_ref, g_ref))
    pl.when(core != 0)(lambda: fetch(g_ref, x_ref))


def sum_kernel(in_ref, out_ref):
    total = jnp.sum(in_ref[...], axis=0)
    for k in range(out_ref.shape[0]):
        out_ref[k] = total


def mix_kernel(core_ref, both_ref, kept_ref, out_ref):
    width = both_ref[0, 0][0:1]
    packed = jnp.exp(-both_ref[1, 0:PACKED].reshape(PACK, LANE) / width)
    both = jnp.concatenate([packed, pltpu.roll(packed, COUNT, 1)], axis=0)
    lane, row = iota((HALF, LANE), 1), iota((HALF, LANE), 0)
    top = jnp.where((lane > row) & (lane < COUNT), both, 0.0)
    low = jnp.where((lane >= HALF) & (lane - HALF < row), pltpu.roll(both, HALF, 1), 0.0)
    half = jnp.concatenate([top, low, jnp.zeros((LANE - COUNT, LANE), jnp.float32)], axis=0)
    eye = jnp.where(iota((LANE, LANE), 0) == iota((LANE, LANE), 1), 1.0, 0.0)
    kernel = (half + half.T + eye)[:COUNT, :COUNT]
    rowsum = jnp.sum(kernel, axis=1, keepdims=True)
    pull = 2.0 / width[:, 0:1]
    own = pull * rowsum
    second = core_ref[...] == 1.0
    parts = jnp.where(second, kept_ref[...], both_ref[1, PACKED:])
    grads = jnp.where(second, both_ref[0, PACKED:], kept_ref[...])
    x = jnp.concatenate([parts[:, s, :] for s in range(SUB)], axis=1)
    g = jnp.concatenate([grads[:, s, :] for s in range(SUB)], axis=1)
    mixed = dot(kernel, g - pull * x, ((1,), (0,)))
    mixed = (mixed + own * x) * (1.0 / COUNT)
    for s in range(SUB):
        out_ref[:, s, :] = mixed[:, s * LANE:(s + 1) * LANE]


def adam_kernel(x_ref, m_ref, v_ref, d_ref, new_x, new_m, new_v, new_d, out_x, out_m, out_v, sems):
    copies = [pltpu.make_async_copy(d_ref, new_d, sems.at[0])]
    copies[0].start()
    rows = x_ref.shape[0] // CHUNKS
    for k in range(CHUNKS):
        part = pl.ds(k * rows, rows)
        direction = d_ref[part]
        first = beta_one * m_ref[part] + (1.0 - beta_one) * direction
        second = beta_two * v_ref[part] + (1.0 - beta_two) * direction * direction
        out_m[part] = first
        out_v[part] = second
        step = first * (learn_rate / (1.0 - beta_one**ADAM_STEP))
        second_hat = second * (1.0 / (1.0 - beta_two**ADAM_STEP))
        out_x[part] = x_ref[part] + step / (jnp.sqrt(second_hat) + adam_eps)
        for i, (src, dst) in enumerate(((out_m, new_m), (out_v, new_v), (out_x, new_x))):
            copy = pltpu.make_async_copy(src.at[part], dst.at[part], sems.at[1 + 3 * k + i])
            copy.start()
            copies.append(copy)
    for copy in copies:
        copy.wait()


IN_VMEM = pl.BlockSpec(memory_space=pltpu.VMEM)
ANYWHERE = pl.BlockSpec(memory_space=pl.ANY)


def call(kernel, out_shape, in_specs, args, out_specs=IN_VMEM, scratch=()):
    args = [
        pltpu.with_memory_space_constraint(a, pltpu.VMEM if s is IN_VMEM else pltpu.HBM)
        for a, s in zip(args, in_specs)
    ]
    return pl.pallas_call(
        kernel, out_shape=out_shape, in_specs=in_specs, out_specs=out_specs, scratch_shapes=list(scratch)
    )(*args)


def vmem(*shape):
    return pltpu.VMEM(shape, jnp.float32)


def tiles(block):
    rows, cols = block.shape
    return (
        block.reshape(rows // SUB, SUB, cols // LANE, LANE)
        .transpose(0, 2, 1, 3)
        .reshape(-1, SUB, LANE)
    )


def untiles(parts, rows, cols):
    return (
        parts.reshape(rows // SUB, cols // LANE, SUB, LANE)
        .transpose(0, 2, 1, 3)
        .reshape(rows, cols)
    )


def exchange(array, axes):
    places = [0]
    for axis in sorted(axes, key="yxz".index):
        size = lax.axis_size(axis)
        step = math.prod(lax.axis_size(a) for a in axes[axes.index(axis) + 1:])
        places = [p + (i + size // 2) % size * step for p in places for i in range(size)]
    return lax.all_to_all(
        array, axes, split_axis=0, concat_axis=0, axis_index_groups=[places], tiled=True
    )


def share(array):
    return lax.all_gather(array, "core", axis=0, tiled=False)


def body(particles, gradients, first_moment, second_moment, spread):
    _, rows, cols = particles.shape
    entries = rows * cols * lax.axis_size("x") * lax.axis_size("core")
    plane = lax.axis_size("y") * lax.axis_size("x")
    depth = lax.axis_size("z")
    core = lax.axis_index("core")
    which = jnp.full((1, SUB, LANE), core.astype(jnp.float32), jnp.float32)
    payload = vmem(PACKED + COUNT, SUB, LANE)
    with jax.named_scope("swap"):
        x, g = tiles(particles[0]), tiles(gradients[0])
        send, own = call(
            choose_kernel, (vmem(COUNT, SUB, LANE),) * 2, [ANYWHERE] * 2, (x, g), out_specs=(IN_VMEM,) * 2,
            scratch=[pltpu.SemaphoreType.DMA((2,))],
        )
        others = share(send)

    def reduce(own, others, spread):
        slab = call(stack_kernel, vmem(COUNT, 2 * SUB, LANE), [IN_VMEM] * 2, (others[0], own))
        slab = exchange(slab, RING)
        part = call(pack_kernel, vmem(plane, PACKED, SUB, LANE), [IN_VMEM], (slab,))
        part = exchange(part, PLANE)
        part = call(sum_kernel, vmem(depth, PACKED, SUB, LANE), [IN_VMEM], (part,))
        part = exchange(part, ("z",))
        return call(
            last_kernel, (payload, vmem(COUNT, SUB, LANE)), [IN_VMEM] * 2, (part, slab), out_specs=(IN_VMEM,) * 2
        )

    def gather(own, others, spread):
        first = exchange(own, ("y",))
        second = exchange(others[1], ("y",))
        slab = call(turn_kernel, vmem(COUNT, 2 * SUB, LANE), [IN_VMEM] * 2, (first, second))
        slab = exchange(slab, ("z",))
        width = jnp.full((SUB, LANE), spread * entries, jnp.float32)
        return call(
            split_kernel, (payload, vmem(COUNT, SUB, LANE)), [IN_VMEM] * 2, (width, slab),
            out_specs=(IN_VMEM,) * 2
        )

    with jax.named_scope("reduce_or_gather"):
        mine, kept = lax.cond(core == 1, reduce, gather, own, others, spread)
        both = share(mine)
    with jax.named_scope("mix"):
        mixed = call(
            mix_kernel, vmem(COUNT, SUB, LANE), [IN_VMEM] * 3, (which, both, kept)
        )
    with jax.named_scope("return_slab"):
        direction = untiles(exchange(mixed, RING), rows, cols)
    with jax.named_scope("adam"):
        block = jax.ShapeDtypeStruct((rows, cols), jnp.float32)
        outs = call(
            adam_kernel, (block,) * 4, [IN_VMEM] * 4,
            (particles[0], first_moment[0], second_moment[0], direction),
            out_specs=(ANYWHERE,) * 4,
            scratch=[vmem(rows, cols)] * 3 + [pltpu.SemaphoreType.DMA((1 + 3 * CHUNKS,))],
        )
    return tuple(out[None] for out in outs)


def solution(mesh):
    split = Mesh(mesh.devices.reshape(16, 4, 4, 2), ("z", "y", "x", "core"))
    block = P(("z", "y"), ("x", "core"), None)
    return jax.shard_map(
        body,
        mesh=split,
        in_specs=(block, block, block, block, P()),
        out_specs=(block, block, block, block),
        check_vma=False,
    )
```
